32 devices in a mesh: groups: 1, fac: 32 (over z, y, x, core).
Axes of the slice: x: 2, y: 2, z: 4, core: 2. Of those that a mesh axis runs over, the one named last changes fastest.
Arguments:
- sky_image: float32 [64, 96, 4096], P(('groups', 'fac')), may hold values from 0 to 18, as said below
- measured_real: float32 [64, 96, 4096], P(('groups', 'fac')), may hold values from -6 to 6
- measured_imaginary: float32 [64, 96, 4096], P(('groups', 'fac')), may hold values from -6 to 6
- sampling_mask: int32 [64, 96, 4096], P(('groups', 'fac')), may hold values 0 or 1
- dual_field: float32 [64, 96, 4096], P('groups', None, 'fac'), may hold values from -6 to 6
Outputs:
- next_image: float32 [64, 96, 4096], P(('groups', 'fac'))
- next_dual: float32 [64, 96, 4096], P('groups', None, 'fac')
The draws below stay inside these ranges and needn't reach their ends.
Inputs may be any that keep to these rules, and one draw needn't show every extreme that they name: `sky_image`: non-negative sky brightness.
All inputs are finite; a program needn't handle non-finite values. No bound on the sum of `sampling_mask` on one device may be relied on, other than what follows from the above.
Results may differ from the reference program's by a relative error of at most 0.00012.
Values sent between devices are 32-bit elements; how exact they have to be, the bound alone decides.
A program may use at most 192 MiB of HBM per device.

```python
import jax
import jax.numpy as jnp
from jax import lax

CHANNELS = 64
COLUMNS = 4096
ROWS = 96
LEVELS = 4
N_FAC = 32


def draw_sky_image(key, part):
    first_key, second_key = jax.random.split(key, 2)
    channel_scale = jnp.exp(jax.random.uniform(first_key, (CHANNELS, 1, 1), jnp.float32, jnp.log(0.3), jnp.log(3.0)))
    pixels = jnp.exp(jax.random.uniform(second_key, (CHANNELS, ROWS, COLUMNS), jnp.float32, jnp.log(0.1), jnp.log(3.0)))
    return channel_scale * pixels


def set_ends(result, rng, low, largest):
    shape = result.shape
    place = [jax.random.randint(jax.random.fold_in(rng, axis), (), 0, shape[axis]) for axis in range(len(shape))]
    result = result.at[tuple(place)].set(low)
    longest = shape.index(max(shape))
    place[longest] = (place[longest] + 1) % shape[longest]
    return result.at[tuple(place)].set(largest)


def block_levels(stream_key, shape, cuts, smallest, largest):
    def one(position, blocks):
        draws = jax.random.uniform(jax.random.fold_in(jax.random.fold_in(stream_key, 6), position), (blocks,), jnp.float32, smallest / len(cuts), largest / len(cuts))
        return jnp.repeat(jnp.exp(draws), shape[position] // blocks).reshape((-1,) + (1,) * (len(shape) - position - 1))

    gain = one(*cuts[0])
    for cut in cuts[1:]:
        gain = gain * one(*cut)
    return gain


def centred(own_key, extent, scale, limit, cuts=(), kind=jnp.bfloat16):
    level = block_levels(own_key, extent, cuts, -0.22, 0.18) if cuts else 1.0
    result = jax.random.normal(own_key, extent, jnp.float32) * scale * level
    return jnp.minimum(jnp.maximum(result, -limit), limit).astype(kind)


def setup_inputs(seed: int = 0, part: int = 0) -> dict:
    splits = jax.random.split(jax.random.key(seed), 6)
    part_keys = jax.random.split(jax.random.fold_in(splits[5], part), 6)
    sky_image = draw_sky_image(jax.random.fold_in(jax.random.fold_in(splits[5], part), 71), part)
    measured_real = centred(part_keys[1], (CHANNELS, ROWS, COLUMNS), 1.0, 6.0, ((0, 32),), jnp.float32)
    measured_imaginary = centred(part_keys[2], (CHANNELS, ROWS, COLUMNS), 1.0, 6.0, ((0, 32),), jnp.float32)
    sampling_mask = set_ends((jax.random.randint(part_keys[3], (CHANNELS, ROWS, COLUMNS), 0, 2) < 1).astype(jnp.int32), jax.random.fold_in(part_keys[3], 1), 0, 1)
    dual_field = centred(part_keys[4], (CHANNELS, ROWS, COLUMNS), 1.0, 6.0, ((2, 32),), jnp.float32)
    return {"sky_image": sky_image, "measured_real": measured_real, "measured_imaginary": measured_imaginary, "sampling_mask": sampling_mask, "dual_field": dual_field}


low_pass = (0.2303778133088964, 0.7148465705529155, 0.6308807679298587, -0.0279837694168599, -0.1870348117190931, 0.0308413818355607, 0.0328830116668852, -0.010597401785069)
high_pass = tuple(((-1) ** tap_index * low_pass[7 - tap_index] for tap_index in range(8)))
primal_step = 0.6
dual_step = 0.8
ball_radius = 12.0

def split_levels(values):
    coarse = values
    details = []
    for level_index in range(LEVELS):
        length = coarse.shape[-1]
        even_index = 2 * jnp.arange(length // 2, dtype=jnp.int32)
        lower = jnp.zeros(coarse.shape[:-1] + (length // 2,), jnp.float32)
        upper = jnp.zeros(coarse.shape[:-1] + (length // 2,), jnp.float32)
        for tap_index in range(8):
            taken = jnp.take(coarse, (even_index + tap_index) % length, axis=-1)
            lower = lower + low_pass[tap_index] * taken
            upper = upper + high_pass[tap_index] * taken
        details.insert(0, upper)
        coarse = lower
    return [coarse] + details

def wavelet_analysis(values):
    turned = jnp.swapaxes(values, 1, 2)
    row_coeffs = jnp.swapaxes(jnp.concatenate(split_levels(turned), -1), 1, 2)
    pieces = split_levels(row_coeffs)
    facet_major = [piece_part.reshape(piece_part.shape[:-1] + (N_FAC, piece_part.shape[-1] // N_FAC)) for piece_part in pieces]
    return jnp.concatenate(facet_major, -1).reshape(values.shape)

def reference(sky_image, measured_real, measured_imaginary, sampling_mask, dual_field):
    spectrum = jnp.fft.fft2(sky_image, axes=(1, 2), norm='ortho')
    weights = sampling_mask.astype(jnp.float32)
    misfit = weights * (spectrum - (measured_real + 1j * measured_imaginary))
    gradient = jnp.real(jnp.fft.ifft2(misfit, axes=(1, 2), norm='ortho'))
    unused_out, pullback = jax.vjp(wavelet_analysis, jnp.zeros_like(dual_field))
    prior_term = pullback(dual_field)[0]
    next_image = jnp.maximum(sky_image - primal_step * (gradient + prior_term), 0.0)
    lifted = dual_field + dual_step * wavelet_analysis(2.0 * next_image - sky_image)
    channel_norm = jnp.sqrt(lax.optimization_barrier(jnp.sum(lifted * lifted, axis=0)))
    next_dual = lifted / jnp.maximum(1.0, channel_norm / ball_radius)
    return (next_image, next_dual)
```

```python
import jax
import jax.numpy as jnp
import ml_dtypes
import numpy as np
from jax import lax
from jax.experimental import pallas as pl
from jax.experimental.pallas import tpu as pltpu
from jax.sharding import PartitionSpec as P

LEVELS = 4
LANES = 128


low_pass = (
    0.2303778133088964,
    0.7148465705529155,
    0.6308807679298587,
    -0.0279837694168599,
    -0.1870348117190931,
    0.0308413818355607,
    0.0328830116668852,
    -0.010597401785069,
)
high_pass = tuple(((-1) ** tap_index * low_pass[7 - tap_index] for tap_index in range(8)))
primal_step = 0.6
dual_step = 0.8
ball_radius = 12.0
vmem_limit = 48 * 1024 * 1024


def split_table(matrix):
    high = np.asarray(matrix, np.float32).astype(ml_dtypes.bfloat16)
    low = (matrix - high.astype(np.float64)).astype(np.float32).astype(ml_dtypes.bfloat16)
    return [jnp.asarray(high), jnp.asarray(low)]


def halves(values):
    high = values.astype(jnp.bfloat16)
    return high, (values - high.astype(jnp.float32)).astype(jnp.bfloat16)


def dot(left, right):
    return jnp.dot(left, right, preferred_element_type=jnp.float32)


def times_table(values, high_ref, low_ref):
    high, low = halves(values)
    return dot(high, high_ref[...]) + (dot(low, high_ref[...]) + dot(high, low_ref[...]))


def table_times(high_ref, low_ref, values):
    high, low = halves(values)
    return dot(high_ref[...], high) + (dot(high_ref[...], low) + dot(low_ref[...], high))


def dft_angles(length):
    grid = np.arange(length)
    return 2.0 * np.pi * (np.outer(grid, grid) % length) / length


def row_tables(rows):
    angles = dft_angles(rows)
    cosine, sine = np.cos(angles) / np.sqrt(rows), np.sin(angles) / np.sqrt(rows)
    return np.concatenate([cosine, -sine], 0), np.concatenate([cosine, -sine], 1)


def lane_tables(tiles):
    lanes = np.arange(LANES)
    point = (LANES // tiles) * (lanes % tiles) + lanes // tiles
    angles = dft_angles(LANES)[point] / 1.0
    scale = 1.0 / np.sqrt(LANES * tiles)
    cosine, sine = np.cos(angles) * scale, np.sin(angles) * scale
    forward = np.block([[cosine, -sine], [sine, cosine]])
    backward = np.block([[cosine.T, sine.T], [-sine.T, cosine.T]])
    return forward, backward


def twist_table(tiles):
    angles = 2.0 * np.pi * np.outer(np.arange(tiles), np.arange(LANES)) / (tiles * LANES)
    both = np.concatenate([np.cos(angles), np.sin(angles)], 1)
    return jnp.asarray(np.repeat(both[:, None, :], 8, 1), jnp.float32)


def transform(points, sign):
    count = len(points)
    if count == 1:
        return points
    even = transform(points[0::2], sign)
    odd = transform(points[1::2], sign)
    half = count // 2
    first, second = [], []
    for index in range(half):
        real, imag = odd[index]
        if index == 0:
            pass
        elif 4 * index == count:
            real, imag = (-sign * imag, sign * real) if sign > 0 else (imag, -real)
        elif 8 * index == count:
            root = float(np.sqrt(0.5))
            real, imag = (
                ((real - imag) * root, (imag + real) * root)
                if sign > 0
                else ((real + imag) * root, (imag - real) * root)
            )
        elif 8 * index == 3 * count:
            root = float(np.sqrt(0.5))
            real, imag = (
                ((-real - imag) * root, (real - imag) * root)
                if sign > 0
                else ((imag - real) * root, (-real - imag) * root)
            )
        else:
            cosine = float(np.cos(2.0 * np.pi * index / count))
            sine = float(sign * np.sin(2.0 * np.pi * index / count))
            real, imag = real * cosine - imag * sine, real * sine + imag * cosine
        first.append((even[index][0] + real, even[index][1] + imag))
        second.append((even[index][0] - real, even[index][1] - imag))
    return first + second


def turn(slabs):
    slabs = list(slabs)
    lane = lax.broadcasted_iota(jnp.int32, slabs[0].shape, 1)
    step = 1
    while step < len(slabs):
        marked = (lane & step) != 0
        for low in range(len(slabs)):
            if low & step:
                continue
            one, other = slabs[low], slabs[low + step]
            slabs[low] = jnp.where(marked, pltpu.roll(other, step, 1), one)
            slabs[low + step] = jnp.where(marked, other, pltpu.roll(one, LANES - step, 1))
        step *= 2
    return slabs


def gradient_kernel(
    sky, meas_re, meas_im, mask, row_fh, row_fl, row_bh, row_bl,
    lane_fh, lane_fl, lane_bh, lane_bl, twist, out, field, real_field,
):
    tiles, rows, _ = real_field.shape
    group = 4

    def tile(index):
        return pl.ds(index * LANES, LANES)

    def turn_in(step, carry):
        here = pl.ds(pl.multiple_of(step * 8, 8), 8)
        for index, slab in enumerate(turn([sky[0, here, tile(t)] for t in range(tiles)])):
            real_field[index, here, :] = slab
        return carry

    lax.fori_loop(0, rows // 8, turn_in, 0)

    def forward(step, carry):
        slabs = [real_field[step * group + i] for i in range(group)]
        both = table_times(row_fh, row_fl, jnp.concatenate(slabs, 1))
        parts = [
            jnp.concatenate([both[:rows, i * LANES : (i + 1) * LANES], both[rows:, i * LANES : (i + 1) * LANES]], 1)
            for i in range(group)
        ]
        result = times_table(jnp.concatenate(parts, 0), lane_fh, lane_fl)
        for i in range(group):
            field[step * group + i] = result[i * rows : (i + 1) * rows]
        return carry

    lax.fori_loop(0, tiles // group, forward, 0)

    def middle(step, carry):
        here = pl.ds(pl.multiple_of(step * 8, 8), 8)
        points = []
        for t in range(tiles):
            real, imag = field[t, here, :LANES], field[t, here, LANES:]
            cosine, sine = twist[t, :, :LANES], twist[t, :, LANES:]
            points.append((real * cosine + imag * sine, imag * cosine - real * sine))
        spectrum = transform(points, -1.0)
        misfit = []
        for t in range(tiles):
            weight = mask[0, here, tile(t)].astype(jnp.float32)
            misfit.append(
                (
                    weight * (spectrum[t][0] - meas_re[0, here, tile(t)]),
                    weight * (spectrum[t][1] - meas_im[0, here, tile(t)]),
                )
            )
        for t, (real, imag) in enumerate(transform(misfit, 1.0)):
            cosine, sine = twist[t, :, :LANES], twist[t, :, LANES:]
            field[t, here, :LANES] = real * cosine - imag * sine
            field[t, here, LANES:] = real * sine + imag * cosine
        return carry

    lax.fori_loop(0, rows // 8, middle, 0)

    def backward(step, carry):
        parts = jnp.concatenate([field[step * group + i] for i in range(group)], 0)
        result = times_table(parts, lane_bh, lane_bl)
        real = [result[i * rows : (i + 1) * rows, :LANES] for i in range(group)]
        imag = [result[i * rows : (i + 1) * rows, LANES:] for i in range(group)]
        both = jnp.concatenate([jnp.concatenate(real, 1), jnp.concatenate(imag, 1)], 0)
        result = table_times(row_bh, row_bl, both)
        for i in range(group):
            real_field[step * group + i] = result[:, i * LANES : (i + 1) * LANES]
        return carry

    lax.fori_loop(0, tiles // group, backward, 0)

    def turn_out(step, carry):
        here = pl.ds(pl.multiple_of(step * 8, 8), 8)
        for index, slab in enumerate(turn([real_field[t, here, :] for t in range(tiles)])):
            out[0, here, tile(index)] = slab
        return carry

    lax.fori_loop(0, rows // 8, turn_out, 0)


def whole(array):
    return pl.BlockSpec(array.shape, lambda c: (0,) * array.ndim)


def channel_block(rows, columns):
    return pl.BlockSpec((1, rows, columns), lambda c: (c, 0, 0))


def data_gradient(sky_image, measured_real, measured_imaginary, sampling_mask):
    channels, rows, columns = sky_image.shape
    tiles = columns // LANES
    row_forward, row_backward = row_tables(rows)
    lane_forward, lane_backward = lane_tables(tiles)
    tables = (
        split_table(row_forward)
        + split_table(row_backward)
        + split_table(lane_forward)
        + split_table(lane_backward)
        + [twist_table(tiles)]
    )
    block = channel_block(rows, columns)
    return pl.pallas_call(
        gradient_kernel,
        name="gradient",
        grid=(channels,),
        in_specs=[block] * 4 + [whole(table) for table in tables],
        out_specs=block,
        out_shape=jax.ShapeDtypeStruct(sky_image.shape, jnp.float32),
        scratch_shapes=[
            pltpu.VMEM((tiles, rows, 2 * LANES), jnp.float32),
            pltpu.VMEM((tiles, rows, LANES), jnp.float32),
        ],
        compiler_params=pltpu.CompilerParams(vmem_limit_bytes=vmem_limit),
        cost_estimate=pl.CostEstimate(
            flops=3 * 2 * channels * rows * columns * 1400, bytes_accessed=20 * channels * rows * columns, transcendentals=0
        ),
    )(sky_image, measured_real, measured_imaginary, sampling_mask, *tables)


def row_matrix(length):
    current = np.eye(length)
    details = []
    for level_index in range(LEVELS):
        width_now = current.shape[0]
        half_size = width_now // 2
        lower = np.zeros((half_size, width_now))
        upper = np.zeros((half_size, width_now))
        for target in range(half_size):
            for tap_index in range(8):
                lower[target, (2 * target + tap_index) % width_now] += low_pass[tap_index]
                upper[target, (2 * target + tap_index) % width_now] += high_pass[tap_index]
        details.insert(0, upper @ current)
        current = lower @ current
    return np.concatenate([current] + details, 0)


def facet_matrix(width):
    long = 4 * width
    full = row_matrix(long)
    picked = []
    start, size = 0, width >> LEVELS
    for level_index in range(LEVELS + 1):
        picked.append(full[start : start + size])
        start = (long >> LEVELS) << level_index
        size = (width >> LEVELS) << level_index
    block = np.concatenate(picked, 0)
    assert np.all(block[:, 2 * width :] == 0.0)
    return block[:, : 2 * width].T


def wavelet_kernel(
    sky, gradient, coefficients, row_sh, row_sl, row_ah, row_al, col_sh, col_sl, col_ah, col_al,
    next_image, analysed, turned,
):
    facets, _, rows, width = coefficients.shape
    group = 4

    def primal(step, carry):
        parts = []
        for i in range(group):
            index = step * group + i
            parts.append(
                jnp.concatenate([coefficients[index, 0], coefficients[(index + facets - 1) % facets, 0]], 1)
            )
        prior = times_table(jnp.concatenate(parts, 0), col_sh, col_sl)
        prior = jnp.concatenate([prior[i * rows : (i + 1) * rows] for i in range(group)], 1)
        prior = table_times(row_sh, row_sl, prior)
        here = pl.ds(pl.multiple_of(step * (group * width), group * width), group * width)
        old = sky[0, :, here]
        new = jnp.maximum(old - primal_step * (gradient[0, :, here] + prior), 0.0)
        next_image[0, :, here] = new
        result = table_times(row_ah, row_al, 2.0 * new - old)
        for i in range(group):
            turned[step * group + i] = result[:, i * width : (i + 1) * width]
        return carry

    lax.fori_loop(0, facets // group, primal, 0)

    def columns(step, carry):
        parts = []
        for i in range(group):
            index = step * group + i
            parts.append(jnp.concatenate([turned[index], turned[(index + 1) % facets]], 1))
        result = times_table(jnp.concatenate(parts, 0), col_ah, col_al)
        for i in range(group):
            analysed[step * group + i, 0] = result[i * rows : (i + 1) * rows]
        return carry

    lax.fori_loop(0, facets // group, columns, 0)


def primal_step_and_analysis(sky_image, gradient, coefficients):
    channels, rows, columns = sky_image.shape
    facets, width = coefficients.shape[0], coefficients.shape[3]
    row_analysis = row_matrix(rows)
    col_analysis = facet_matrix(width)
    col_synthesis = np.concatenate([col_analysis[:width].T, col_analysis[width:].T], 0)
    tables = (
        split_table(row_analysis.T)
        + split_table(row_analysis)
        + split_table(col_synthesis)
        + split_table(col_analysis)
    )
    block = channel_block(rows, columns)
    facet_block = pl.BlockSpec((facets, 1, rows, width), lambda c: (0, c, 0, 0))
    return pl.pallas_call(
        wavelet_kernel,
        name="wavelet",
        grid=(channels,),
        in_specs=[block, block, facet_block] + [whole(table) for table in tables],
        out_specs=[block, facet_block],
        out_shape=[
            jax.ShapeDtypeStruct(sky_image.shape, jnp.float32),
            jax.ShapeDtypeStruct(coefficients.shape, jnp.float32),
        ],
        scratch_shapes=[pltpu.VMEM((facets, rows, width), jnp.float32)],
        compiler_params=pltpu.CompilerParams(vmem_limit_bytes=vmem_limit),
        cost_estimate=pl.CostEstimate(
            flops=3 * 2 * channels * rows * columns * 700, bytes_accessed=20 * channels * rows * columns, transcendentals=0
        ),
    )(sky_image, gradient, coefficients, *tables)


def shrink_kernel(dual, update, out):
    total = jnp.zeros(dual.shape[1:], jnp.float32)
    for channel in range(dual.shape[0]):
        lifted = dual[channel] + dual_step * update[channel]
        out[channel] = lifted
        total = total + lifted * lifted
    factor = 1.0 / jnp.maximum(1.0, jnp.sqrt(total) / ball_radius)
    for channel in range(dual.shape[0]):
        out[channel] = out[channel] * factor


def shrink(dual, update):
    channels, rows, width = dual.shape
    block = pl.BlockSpec((channels, 8, width), lambda r: (0, r, 0))
    return pl.pallas_call(
        shrink_kernel,
        name="shrink",
        grid=(rows // 8,),
        in_specs=[block, block],
        out_specs=block,
        out_shape=jax.ShapeDtypeStruct(dual.shape, jnp.float32),
        compiler_params=pltpu.CompilerParams(vmem_limit_bytes=vmem_limit),
        cost_estimate=pl.CostEstimate(flops=5 * dual.size, bytes_accessed=12 * dual.size, transcendentals=0),
    )(dual, update)


def shards(sky_image, measured_real, measured_imaginary, sampling_mask, dual_field):
    channels, rows, columns = sky_image.shape
    facets = lax.axis_size("fac")
    local_dual = lax.all_to_all(dual_field, "fac", split_axis=0, concat_axis=0, tiled=True)
    gradient = data_gradient(sky_image, measured_real, measured_imaginary, sampling_mask)
    next_image, analysed = primal_step_and_analysis(
        sky_image, gradient, local_dual.reshape(facets, channels, rows, columns // facets)
    )
    update = lax.all_to_all(
        analysed.reshape(dual_field.shape), "fac", split_axis=0, concat_axis=0, tiled=True
    )
    return (next_image, shrink(dual_field, update))


def solution(mesh):
    return jax.shard_map(
        shards,
        mesh=mesh,
        in_specs=(
            P(("groups", "fac"), None, None),
            P(("groups", "fac"), None, None),
            P(("groups", "fac"), None, None),
            P(("groups", "fac"), None, None),
            P("groups", None, "fac"),
        ),
        out_specs=(P(("groups", "fac"), None, None), P("groups", None, "fac")),
        check_vma=False,
    )
```

```python
import jax
import jax.numpy as jnp
import ml_dtypes
import numpy as np
from jax import lax
from jax.experimental import pallas as pl
from jax.experimental.pallas import tpu as pltpu
from jax.sharding import PartitionSpec as P

LEVELS = 4
LANES = 128


low_pass = (
    0.2303778133088964,
    0.7148465705529155,
    0.6308807679298587,
    -0.0279837694168599,
    -0.1870348117190931,
    0.0308413818355607,
    0.0328830116668852,
    -0.010597401785069,
)
high_pass = tuple(((-1) ** tap_index * low_pass[7 - tap_index] for tap_index in range(8)))
primal_step = 0.6
dual_step = 0.8
ball_radius = 12.0
vmem_limit = 32 * 1024 * 1024


def split_table(matrix):
    high = np.asarray(matrix, np.float32).astype(ml_dtypes.bfloat16)
    low = (matrix - high.astype(np.float64)).astype(np.float32).astype(ml_dtypes.bfloat16)
    return [jnp.asarray(high), jnp.asarray(low)]


def halves(values):
    high = values.astype(jnp.bfloat16)
    return high, (values - high.astype(jnp.float32)).astype(jnp.bfloat16)


def dot(left, right):
    return jnp.dot(left, right, preferred_element_type=jnp.float32)


def times_table(values, high_ref, low_ref):
    high, low = halves(values)
    return dot(high, high_ref[...]) + (dot(low, high_ref[...]) + dot(high, low_ref[...]))


def table_times(high_ref, low_ref, values):
    high, low = halves(values)
    return dot(high_ref[...], high) + (dot(high_ref[...], low) + dot(low_ref[...], high))


def dft_angles(length):
    grid = np.arange(length)
    return 2.0 * np.pi * (np.outer(grid, grid) % length) / length


def row_tables(rows):
    angles = dft_angles(rows)
    cosine, sine = np.cos(angles) / np.sqrt(rows), np.sin(angles) / np.sqrt(rows)
    return np.concatenate([cosine, -sine], 0), np.concatenate([cosine, -sine], 1)


def lane_tables(tiles):
    lanes = np.arange(LANES)
    point = (LANES // tiles) * (lanes % tiles) + lanes // tiles
    angles = dft_angles(LANES)[point] / 1.0
    scale = 1.0 / np.sqrt(LANES * tiles)
    cosine, sine = np.cos(angles) * scale, np.sin(angles) * scale
    forward = np.block([[cosine, -sine], [sine, cosine]])
    backward = np.block([[cosine.T, sine.T], [-sine.T, cosine.T]])
    return forward, backward


def twist_table(tiles):
    angles = 2.0 * np.pi * np.outer(np.arange(tiles), np.arange(LANES)) / (tiles * LANES)
    both = np.concatenate([np.cos(angles), np.sin(angles)], 1)
    return jnp.asarray(np.repeat(both[:, None, :], 8, 1), jnp.float32)


def transform(points, sign):
    count = len(points)
    if count == 1:
        return points
    even = transform(points[0::2], sign)
    odd = transform(points[1::2], sign)
    half = count // 2
    first, second = [], []
    for index in range(half):
        real, imag = odd[index]
        if index == 0:
            pass
        elif 4 * index == count:
            real, imag = (-sign * imag, sign * real) if sign > 0 else (imag, -real)
        elif 8 * index == count:
            root = float(np.sqrt(0.5))
            real, imag = (
                ((real - imag) * root, (imag + real) * root)
                if sign > 0
                else ((real + imag) * root, (imag - real) * root)
            )
        elif 8 * index == 3 * count:
            root = float(np.sqrt(0.5))
            real, imag = (
                ((-real - imag) * root, (real - imag) * root)
                if sign > 0
                else ((imag - real) * root, (-real - imag) * root)
            )
        else:
            cosine = float(np.cos(2.0 * np.pi * index / count))
            sine = float(sign * np.sin(2.0 * np.pi * index / count))
            real, imag = real * cosine - imag * sine, real * sine + imag * cosine
        first.append((even[index][0] + real, even[index][1] + imag))
        second.append((even[index][0] - real, even[index][1] - imag))
    return first + second


def turn(slabs):
    slabs = list(slabs)
    lane = lax.broadcasted_iota(jnp.int32, slabs[0].shape, 1)
    step = 1
    while step < len(slabs):
        marked = (lane & step) != 0
        for low in range(len(slabs)):
            if low & step:
                continue
            one, other = slabs[low], slabs[low + step]
            slabs[low] = jnp.where(marked, pltpu.roll(other, step, 1), one)
            slabs[low + step] = jnp.where(marked, other, pltpu.roll(one, LANES - step, 1))
        step *= 2
    return slabs


def gradient_kernel(
    sky, meas_re, meas_im, mask, row_fh, row_fl, row_bh, row_bl,
    lane_fh, lane_fl, lane_bh, lane_bl, twist, *rest,
):
    out, field, real_field = rest[-3:]
    tiles, rows, _ = real_field.shape
    group = 4

    def tile(index):
        return pl.ds(index * LANES, LANES)

    def turn_in(step, carry):
        here = pl.ds(pl.multiple_of(step * 8, 8), 8)
        for index, slab in enumerate(turn([sky[0, here, tile(t)] for t in range(tiles)])):
            real_field[index, here, :] = slab
        return carry

    lax.fori_loop(0, rows // 8, turn_in, 0)

    def forward(step, carry):
        slabs = [real_field[step * group + i] for i in range(group)]
        both = table_times(row_fh, row_fl, jnp.concatenate(slabs, 1))
        parts = [
            jnp.concatenate([both[:rows, i * LANES : (i + 1) * LANES], both[rows:, i * LANES : (i + 1) * LANES]], 1)
            for i in range(group)
        ]
        result = times_table(jnp.concatenate(parts, 0), lane_fh, lane_fl)
        for i in range(group):
            field[step * group + i] = result[i * rows : (i + 1) * rows]
        return carry

    lax.fori_loop(0, tiles // group, forward, 0)

    def middle(step, carry):
        here = pl.ds(pl.multiple_of(step * 8, 8), 8)
        points = []
        for t in range(tiles):
            real, imag = field[t, here, :LANES], field[t, here, LANES:]
            cosine, sine = twist[t, :, :LANES], twist[t, :, LANES:]
            points.append((real * cosine + imag * sine, imag * cosine - real * sine))
        spectrum = transform(points, -1.0)
        misfit = []
        for t in range(tiles):
            weight = mask[0, here, tile(t)].astype(jnp.float32)
            misfit.append(
                (
                    weight * (spectrum[t][0] - meas_re[0, here, tile(t)]),
                    weight * (spectrum[t][1] - meas_im[0, here, tile(t)]),
                )
            )
        for t, (real, imag) in enumerate(transform(misfit, 1.0)):
            cosine, sine = twist[t, :, :LANES], twist[t, :, LANES:]
            field[t, here, :LANES] = real * cosine - imag * sine
            field[t, here, LANES:] = real * sine + imag * cosine
        return carry

    lax.fori_loop(0, rows // 8, middle, 0)

    def backward(step, carry):
        parts = jnp.concatenate([field[step * group + i] for i in range(group)], 0)
        result = times_table(parts, lane_bh, lane_bl)
        real = [result[i * rows : (i + 1) * rows, :LANES] for i in range(group)]
        imag = [result[i * rows : (i + 1) * rows, LANES:] for i in range(group)]
        both = jnp.concatenate([jnp.concatenate(real, 1), jnp.concatenate(imag, 1)], 0)
        result = table_times(row_bh, row_bl, both)
        for i in range(group):
            real_field[step * group + i] = result[:, i * LANES : (i + 1) * LANES]
        return carry

    lax.fori_loop(0, tiles // group, backward, 0)

    def turn_out(step, carry):
        here = pl.ds(pl.multiple_of(step * 8, 8), 8)
        for index, slab in enumerate(turn([real_field[t, here, :] for t in range(tiles)])):
            out[0, here, tile(index)] = slab
        return carry

    lax.fori_loop(0, rows // 8, turn_out, 0)


def whole(array):
    return pl.BlockSpec(array.shape, lambda c: (0,) * array.ndim)


def channel_block(rows, columns, channel):
    return pl.BlockSpec((1, rows, columns), lambda c: (channel, 0, 0))


def data_gradient(sky_image, measured_real, measured_imaginary, sampling_mask, channel, after):
    channels, rows, columns = sky_image.shape
    tiles = columns // LANES
    row_forward, row_backward = row_tables(rows)
    lane_forward, lane_backward = lane_tables(tiles)
    tables = (
        split_table(row_forward)
        + split_table(row_backward)
        + split_table(lane_forward)
        + split_table(lane_backward)
        + [twist_table(tiles)]
    )
    block = channel_block(rows, columns, channel)
    return pl.pallas_call(
        gradient_kernel,
        name="gradient",
        grid=(1,),
        in_specs=[block] * 4
        + [whole(table) for table in tables]
        + [pl.BlockSpec(memory_space=pl.ANY)] * len(after),
        out_specs=channel_block(rows, columns, 0),
        out_shape=jax.ShapeDtypeStruct((1, rows, columns), jnp.float32),
        scratch_shapes=[
            pltpu.VMEM((tiles, rows, 2 * LANES), jnp.float32),
            pltpu.VMEM((tiles, rows, LANES), jnp.float32),
        ],
        compiler_params=pltpu.CompilerParams(vmem_limit_bytes=vmem_limit),
        cost_estimate=pl.CostEstimate(
            flops=3 * 2 * rows * columns * 1400, bytes_accessed=20 * rows * columns, transcendentals=0
        ),
    )(sky_image, measured_real, measured_imaginary, sampling_mask, *tables, *after)


def row_matrix(length):
    current = np.eye(length)
    details = []
    for level_index in range(LEVELS):
        width_now = current.shape[0]
        half_size = width_now // 2
        lower = np.zeros((half_size, width_now))
        upper = np.zeros((half_size, width_now))
        for target in range(half_size):
            for tap_index in range(8):
                lower[target, (2 * target + tap_index) % width_now] += low_pass[tap_index]
                upper[target, (2 * target + tap_index) % width_now] += high_pass[tap_index]
        details.insert(0, upper @ current)
        current = lower @ current
    return np.concatenate([current] + details, 0)


def facet_matrix(width):
    long = 4 * width
    full = row_matrix(long)
    picked = []
    start, size = 0, width >> LEVELS
    for level_index in range(LEVELS + 1):
        picked.append(full[start : start + size])
        start = (long >> LEVELS) << level_index
        size = (width >> LEVELS) << level_index
    block = np.concatenate(picked, 0)
    assert np.all(block[:, 2 * width :] == 0.0)
    return block[:, : 2 * width].T


def wavelet_kernel(
    sky, gradient, coefficients, row_sh, row_sl, row_ah, row_al, col_sh, col_sl, col_ah, col_al,
    *rest,
):
    next_image, analysed, turned = rest[-3:]
    facets, rows, width = coefficients.shape
    group = 4

    def primal(step, carry):
        parts = []
        for i in range(group):
            index = step * group + i
            parts.append(
                jnp.concatenate([coefficients[index], coefficients[(index + facets - 1) % facets]], 1)
            )
        prior = times_table(jnp.concatenate(parts, 0), col_sh, col_sl)
        prior = jnp.concatenate([prior[i * rows : (i + 1) * rows] for i in range(group)], 1)
        prior = table_times(row_sh, row_sl, prior)
        here = pl.ds(pl.multiple_of(step * (group * width), group * width), group * width)
        old = sky[0, :, here]
        new = jnp.maximum(old - primal_step * (gradient[0, :, here] + prior), 0.0)
        next_image[0, :, here] = new
        result = table_times(row_ah, row_al, 2.0 * new - old)
        for i in range(group):
            turned[step * group + i] = result[:, i * width : (i + 1) * width]
        return carry

    lax.fori_loop(0, facets // group, primal, 0)

    def columns(step, carry):
        parts = []
        for i in range(group):
            index = step * group + i
            parts.append(jnp.concatenate([turned[index], turned[(index + 1) % facets]], 1))
        result = times_table(jnp.concatenate(parts, 0), col_ah, col_al)
        for i in range(group):
            analysed[step * group + i] = result[i * rows : (i + 1) * rows]
        return carry

    lax.fori_loop(0, facets // group, columns, 0)


def primal_step_and_analysis(sky_image, gradient, coefficients, channel, image):
    channels, rows, columns = sky_image.shape
    facets, width = coefficients.shape[0], coefficients.shape[2]
    row_analysis = row_matrix(rows)
    col_analysis = facet_matrix(width)
    col_synthesis = np.concatenate([col_analysis[:width].T, col_analysis[width:].T], 0)
    tables = (
        split_table(row_analysis.T)
        + split_table(row_analysis)
        + split_table(col_synthesis)
        + split_table(col_analysis)
    )
    block = channel_block(rows, columns, channel)
    operands = [sky_image, gradient, coefficients] + tables
    return pl.pallas_call(
        wavelet_kernel,
        name="wavelet",
        grid=(1,),
        in_specs=[block, channel_block(rows, columns, 0), whole(coefficients)]
        + [whole(table) for table in tables]
        + [pl.BlockSpec(memory_space=pl.ANY)] * len(image),
        out_specs=[block, whole(coefficients)],
        input_output_aliases={len(operands): 0} if image else {},
        out_shape=[
            jax.ShapeDtypeStruct(sky_image.shape, jnp.float32),
            jax.ShapeDtypeStruct(coefficients.shape, jnp.float32),
        ],
        scratch_shapes=[pltpu.VMEM((facets, rows, width), jnp.float32)],
        compiler_params=pltpu.CompilerParams(vmem_limit_bytes=vmem_limit),
        cost_estimate=pl.CostEstimate(
            flops=3 * 2 * rows * columns * 700, bytes_accessed=20 * rows * columns, transcendentals=0
        ),
    )(*operands, *image)


def shrink_kernel(dual, *refs):
    updates, out = refs[:-1], refs[-1]
    total = jnp.zeros(dual.shape[2:], jnp.float32)
    for channel, update in enumerate(updates):
        for source in range(dual.shape[0]):
            lifted = dual[source, channel] + dual_step * update[source]
            out[source, channel] = lifted
            total = total + lifted * lifted
    factor = 1.0 / jnp.maximum(1.0, jnp.sqrt(total) / ball_radius)
    for channel in range(dual.shape[1]):
        for source in range(dual.shape[0]):
            out[source, channel] = out[source, channel] * factor


def shrink(dual, updates):
    sources, channels, rows, width = dual.shape
    block = pl.BlockSpec((sources, channels, 8, width), lambda r: (0, 0, r, 0))
    part = pl.BlockSpec((sources, 8, width), lambda r: (0, r, 0))
    return pl.pallas_call(
        shrink_kernel,
        name="shrink",
        grid=(rows // 8,),
        in_specs=[block] + [part] * channels,
        out_specs=block,
        out_shape=jax.ShapeDtypeStruct(dual.shape, jnp.float32),
        compiler_params=pltpu.CompilerParams(vmem_limit_bytes=12 * 1024 * 1024),
        cost_estimate=pl.CostEstimate(flops=5 * dual.size, bytes_accessed=12 * dual.size, transcendentals=0),
    )(dual, *updates)


def exchange(blocks):
    return lax.all_to_all(blocks, "fac", split_axis=0, concat_axis=0, tiled=True)


def shards(sky_image, measured_real, measured_imaginary, sampling_mask, dual_field):
    channels, rows, columns = sky_image.shape
    facets = lax.axis_size("fac")
    dual = dual_field.reshape(facets, channels, rows, columns // facets)
    local_dual = [exchange(dual[:, channel]) for channel in range(channels)]
    image, updates, after = [], [], []
    for channel in range(channels):
        gradient = data_gradient(
            sky_image, measured_real, measured_imaginary, sampling_mask, channel, after
        )
        next_image, analysed = primal_step_and_analysis(
            sky_image, gradient, local_dual[channel], channel, image
        )
        updates.append(exchange(analysed))
        image, after = [next_image], [analysed]
    return (image[0], shrink(dual, updates).reshape(dual_field.shape))


def solution(mesh):
    return jax.shard_map(
        shards,
        mesh=mesh,
        in_specs=(
            P(("groups", "fac"), None, None),
            P(("groups", "fac"), None, None),
            P(("groups", "fac"), None, None),
            P(("groups", "fac"), None, None),
            P("groups", None, "fac"),
        ),
        out_specs=(P(("groups", "fac"), None, None), P("groups", None, "fac")),
        check_vma=False,
    )
```

```python
import jax
import jax.numpy as jnp
import ml_dtypes
import numpy as np
from jax import lax
from jax.experimental import pallas as pl
from jax.experimental.pallas import tpu as pltpu
from jax.sharding import PartitionSpec as P

LEVELS = 4
LANES = 128


low_pass = (
    0.2303778133088964,
    0.7148465705529155,
    0.6308807679298587,
    -0.0279837694168599,
    -0.1870348117190931,
    0.0308413818355607,
    0.0328830116668852,
    -0.010597401785069,
)
high_pass = tuple(((-1) ** tap_index * low_pass[7 - tap_index] for tap_index in range(8)))
primal_step = 0.6
dual_step = 0.8
ball_radius = 12.0
vmem_limit = 48 * 1024 * 1024


def split_table(matrix):
    high = np.asarray(matrix, np.float32).astype(ml_dtypes.bfloat16)
    low = (matrix - high.astype(np.float64)).astype(np.float32).astype(ml_dtypes.bfloat16)
    return [jnp.asarray(high), jnp.asarray(low)]


def halves(values):
    high = values.astype(jnp.bfloat16)
    return high, (values - high.astype(jnp.float32)).astype(jnp.bfloat16)


def dot(left, right):
    return jnp.dot(left, right, preferred_element_type=jnp.float32)


def times_table(values, high_ref, low_ref):
    high, low = halves(values)
    return dot(high, high_ref[...]) + (dot(low, high_ref[...]) + dot(high, low_ref[...]))


def table_times(high_ref, low_ref, values):
    high, low = halves(values)
    return dot(high_ref[...], high) + (dot(high_ref[...], low) + dot(low_ref[...], high))


def dft_angles(length):
    grid = np.arange(length)
    return 2.0 * np.pi * (np.outer(grid, grid) % length) / length


def row_tables(rows):
    angles = dft_angles(rows)
    cosine, sine = np.cos(angles) / np.sqrt(rows), np.sin(angles) / np.sqrt(rows)
    return np.concatenate([cosine, -sine], 0), np.concatenate([cosine, -sine], 1)


def lane_tables(tiles):
    lanes = np.arange(LANES)
    point = (LANES // tiles) * (lanes % tiles) + lanes // tiles
    angles = dft_angles(LANES)[point] / 1.0
    scale = 1.0 / np.sqrt(LANES * tiles)
    cosine, sine = np.cos(angles) * scale, np.sin(angles) * scale
    forward = np.block([[cosine, -sine], [sine, cosine]])
    backward = np.block([[cosine.T, sine.T], [-sine.T, cosine.T]])
    return forward, backward


def twist_table(tiles):
    angles = 2.0 * np.pi * np.outer(np.arange(tiles), np.arange(LANES)) / (tiles * LANES)
    both = np.concatenate([np.cos(angles), np.sin(angles)], 1)
    return jnp.asarray(np.repeat(both[:, None, :], 8, 1), jnp.float32)


def transform(points, sign):
    count = len(points)
    if count == 1:
        return points
    even = transform(points[0::2], sign)
    odd = transform(points[1::2], sign)
    half = count // 2
    first, second = [], []
    for index in range(half):
        real, imag = odd[index]
        if index == 0:
            pass
        elif 4 * index == count:
            real, imag = (-sign * imag, sign * real) if sign > 0 else (imag, -real)
        elif 8 * index == count:
            root = float(np.sqrt(0.5))
            real, imag = (
                ((real - imag) * root, (imag + real) * root)
                if sign > 0
                else ((real + imag) * root, (imag - real) * root)
            )
        elif 8 * index == 3 * count:
            root = float(np.sqrt(0.5))
            real, imag = (
                ((-real - imag) * root, (real - imag) * root)
                if sign > 0
                else ((imag - real) * root, (-real - imag) * root)
            )
        else:
            cosine = float(np.cos(2.0 * np.pi * index / count))
            sine = float(sign * np.sin(2.0 * np.pi * index / count))
            real, imag = real * cosine - imag * sine, real * sine + imag * cosine
        first.append((even[index][0] + real, even[index][1] + imag))
        second.append((even[index][0] - real, even[index][1] - imag))
    return first + second


def turn(slabs):
    slabs = list(slabs)
    lane = lax.broadcasted_iota(jnp.int32, slabs[0].shape, 1)
    step = 1
    while step < len(slabs):
        marked = (lane & step) != 0
        for low in range(len(slabs)):
            if low & step:
                continue
            one, other = slabs[low], slabs[low + step]
            slabs[low] = jnp.where(marked, pltpu.roll(other, step, 1), one)
            slabs[low + step] = jnp.where(marked, other, pltpu.roll(one, LANES - step, 1))
        step *= 2
    return slabs


def gradient_kernel(
    sky, meas_re, meas_im, mask, row_fh, row_fl, row_bh, row_bl,
    lane_fh, lane_fl, lane_bh, lane_bl, twist, out, field, real_field,
):
    tiles, rows, _ = real_field.shape
    group = 4

    def tile(index):
        return pl.ds(index * LANES, LANES)

    def turn_in(step, carry):
        here = pl.ds(pl.multiple_of(step * 8, 8), 8)
        for index, slab in enumerate(turn([sky[0, here, tile(t)] for t in range(tiles)])):
            real_field[index, here, :] = slab
        return carry

    lax.fori_loop(0, rows // 8, turn_in, 0)

    def forward(step, carry):
        slabs = [real_field[step * group + i] for i in range(group)]
        both = table_times(row_fh, row_fl, jnp.concatenate(slabs, 1))
        parts = [
            jnp.concatenate([both[:rows, i * LANES : (i + 1) * LANES], both[rows:, i * LANES : (i + 1) * LANES]], 1)
            for i in range(group)
        ]
        result = times_table(jnp.concatenate(parts, 0), lane_fh, lane_fl)
        for i in range(group):
            field[step * group + i] = result[i * rows : (i + 1) * rows]
        return carry

    lax.fori_loop(0, tiles // group, forward, 0)

    def middle(step, carry):
        here = pl.ds(pl.multiple_of(step * 8, 8), 8)
        points = []
        for t in range(tiles):
            real, imag = field[t, here, :LANES], field[t, here, LANES:]
            cosine, sine = twist[t, :, :LANES], twist[t, :, LANES:]
            points.append((real * cosine + imag * sine, imag * cosine - real * sine))
        spectrum = transform(points, -1.0)
        misfit = []
        for t in range(tiles):
            weight = mask[0, here, tile(t)].astype(jnp.float32)
            misfit.append(
                (
                    weight * (spectrum[t][0] - meas_re[0, here, tile(t)]),
                    weight * (spectrum[t][1] - meas_im[0, here, tile(t)]),
                )
            )
        for t, (real, imag) in enumerate(transform(misfit, 1.0)):
            cosine, sine = twist[t, :, :LANES], twist[t, :, LANES:]
            field[t, here, :LANES] = real * cosine - imag * sine
            field[t, here, LANES:] = real * sine + imag * cosine
        return carry

    lax.fori_loop(0, rows // 8, middle, 0)

    def backward(step, carry):
        parts = jnp.concatenate([field[step * group + i] for i in range(group)], 0)
        result = times_table(parts, lane_bh, lane_bl)
        real = [result[i * rows : (i + 1) * rows, :LANES] for i in range(group)]
        imag = [result[i * rows : (i + 1) * rows, LANES:] for i in range(group)]
        both = jnp.concatenate([jnp.concatenate(real, 1), jnp.concatenate(imag, 1)], 0)
        result = table_times(row_bh, row_bl, both)
        for i in range(group):
            real_field[step * group + i] = result[:, i * LANES : (i + 1) * LANES]
        return carry

    lax.fori_loop(0, tiles // group, backward, 0)

    def turn_out(step, carry):
        here = pl.ds(pl.multiple_of(step * 8, 8), 8)
        for index, slab in enumerate(turn([real_field[t, here, :] for t in range(tiles)])):
            out[0, here, tile(index)] = slab
        return carry

    lax.fori_loop(0, rows // 8, turn_out, 0)


def whole(array):
    return pl.BlockSpec(array.shape, lambda c: (0,) * array.ndim)


def channel_block(rows, columns):
    return pl.BlockSpec((1, rows, columns), lambda c: (c, 0, 0))


def data_gradient(sky_image, measured_real, measured_imaginary, sampling_mask):
    channels, rows, columns = sky_image.shape
    tiles = columns // LANES
    row_forward, row_backward = row_tables(rows)
    lane_forward, lane_backward = lane_tables(tiles)
    tables = (
        split_table(row_forward)
        + split_table(row_backward)
        + split_table(lane_forward)
        + split_table(lane_backward)
        + [twist_table(tiles)]
    )
    block = channel_block(rows, columns)
    return pl.pallas_call(
        gradient_kernel,
        name="gradient",
        grid=(channels,),
        in_specs=[block] * 4 + [whole(table) for table in tables],
        out_specs=block,
        out_shape=jax.ShapeDtypeStruct(sky_image.shape, jnp.float32),
        scratch_shapes=[
            pltpu.VMEM((tiles, rows, 2 * LANES), jnp.float32),
            pltpu.VMEM((tiles, rows, LANES), jnp.float32),
        ],
        compiler_params=pltpu.CompilerParams(vmem_limit_bytes=vmem_limit),
        cost_estimate=pl.CostEstimate(
            flops=3 * 2 * channels * rows * columns * 1400, bytes_accessed=20 * channels * rows * columns, transcendentals=0
        ),
    )(sky_image, measured_real, measured_imaginary, sampling_mask, *tables)


def row_matrix(length):
    current = np.eye(length)
    details = []
    for level_index in range(LEVELS):
        width_now = current.shape[0]
        half_size = width_now // 2
        lower = np.zeros((half_size, width_now))
        upper = np.zeros((half_size, width_now))
        for target in range(half_size):
            for tap_index in range(8):
                lower[target, (2 * target + tap_index) % width_now] += low_pass[tap_index]
                upper[target, (2 * target + tap_index) % width_now] += high_pass[tap_index]
        details.insert(0, upper @ current)
        current = lower @ current
    return np.concatenate([current] + details, 0)


def facet_matrix(width):
    long = 4 * width
    full = row_matrix(long)
    picked = []
    start, size = 0, width >> LEVELS
    for level_index in range(LEVELS + 1):
        picked.append(full[start : start + size])
        start = (long >> LEVELS) << level_index
        size = (width >> LEVELS) << level_index
    block = np.concatenate(picked, 0)
    assert np.all(block[:, 2 * width :] == 0.0)
    return block[:, : 2 * width].T


def wavelet_kernel(
    sky, gradient, coefficients, row_sh, row_sl, row_ah, row_al, col_sh, col_sl, col_ah, col_al,
    next_image, received, turned, analysed, send_sem, recv_sem, own_sem,
):
    facets, channels, rows, width = coefficients.shape
    group = 4
    chunks = facets // group
    me = lax.axis_index("fac")
    mesh_id = pl.DeviceIdType.MESH

    barrier = pltpu.get_barrier_semaphore()

    def greet(shift, carry):
        pl.semaphore_signal(
            barrier, inc=1, device_id={"fac": (me + shift) % facets}, device_id_type=mesh_id
        )
        return carry

    lax.fori_loop(1, facets, greet, 0)
    pl.semaphore_wait(barrier, facets - 1)

    def copy_to(facet, shift):
        return pltpu.make_async_remote_copy(
            src_ref=analysed.at[facet],
            dst_ref=received.at[me],
            send_sem=send_sem.at[shift],
            recv_sem=recv_sem.at[shift],
            device_id={"fac": facet},
            device_id_type=mesh_id,
        )

    def chunk_at(step):
        return (me // group + chunks // 2 + step) % chunks

    def primal(step):
        chunk = chunk_at(step)
        here = pl.ds(pl.multiple_of(chunk * (group * width), group * width), group * width)
        for channel in range(channels):
            parts = []
            for i in range(group):
                index = chunk * group + i
                parts.append(
                    jnp.concatenate(
                        [coefficients[index, channel], coefficients[(index + facets - 1) % facets, channel]], 1
                    )
                )
            prior = times_table(jnp.concatenate(parts, 0), col_sh, col_sl)
            prior = jnp.concatenate([prior[i * rows : (i + 1) * rows] for i in range(group)], 1)
            prior = table_times(row_sh, row_sl, prior)
            old = sky[channel, :, here]
            new = jnp.maximum(old - primal_step * (gradient[channel, :, here] + prior), 0.0)
            next_image[channel, :, here] = new
            result = table_times(row_ah, row_al, 2.0 * new - old)
            for i in range(group):
                turned[chunk * group + i, channel] = result[:, i * width : (i + 1) * width]

    def columns(step):
        chunk = chunk_at(step)
        for channel in range(channels):
            parts = []
            for i in range(group):
                index = chunk * group + i
                parts.append(
                    jnp.concatenate([turned[index, channel], turned[(index + 1) % facets, channel]], 1)
                )
            result = times_table(jnp.concatenate(parts, 0), col_ah, col_al)
            for i in range(group):
                analysed[chunk * group + i, channel] = result[i * rows : (i + 1) * rows]
        for i in range(group):
            facet = chunk * group + i

            @pl.when(facet != me)
            def _():
                copy_to(facet, (facet - me + facets) % facets).start()

    primal(0)

    def both(step, carry):
        primal(step)
        columns(step - 1)
        return carry

    lax.fori_loop(1, chunks, both, 0)
    columns(chunks - 1)
    own = pltpu.make_async_copy(analysed.at[me], received.at[me], own_sem)
    own.start()
    own.wait()

    def finish(shift, carry):
        to = (me + shift) % facets
        copy_to(to, shift).wait_send()
        pltpu.make_async_remote_copy(
            src_ref=analysed.at[to],
            dst_ref=received.at[(me + facets - shift) % facets],
            send_sem=send_sem.at[shift],
            recv_sem=recv_sem.at[shift],
            device_id={"fac": to},
            device_id_type=mesh_id,
        ).wait_recv()
        return carry

    lax.fori_loop(1, facets, finish, 0)


def primal_step_and_analysis(sky_image, gradient, coefficients):
    channels, rows, columns = sky_image.shape
    facets, width = coefficients.shape[0], coefficients.shape[3]
    row_analysis = row_matrix(rows)
    col_analysis = facet_matrix(width)
    col_synthesis = np.concatenate([col_analysis[:width].T, col_analysis[width:].T], 0)
    tables = (
        split_table(row_analysis.T)
        + split_table(row_analysis)
        + split_table(col_synthesis)
        + split_table(col_analysis)
    )
    operands = [sky_image, gradient, coefficients] + tables
    vmem = pl.BlockSpec(memory_space=pltpu.VMEM)
    return pl.pallas_call(
        wavelet_kernel,
        name="wavelet",
        in_specs=[vmem] * len(operands),
        out_specs=[vmem, pl.BlockSpec(memory_space=pl.ANY)],
        out_shape=[
            jax.ShapeDtypeStruct(sky_image.shape, jnp.float32),
            jax.ShapeDtypeStruct(coefficients.shape, jnp.float32),
        ],
        scratch_shapes=[
            pltpu.VMEM((facets, channels, rows, width), jnp.float32),
            pltpu.VMEM((facets, channels, rows, width), jnp.float32),
            pltpu.SemaphoreType.DMA((facets,)),
            pltpu.SemaphoreType.DMA((facets,)),
            pltpu.SemaphoreType.DMA,
        ],
        compiler_params=pltpu.CompilerParams(
            vmem_limit_bytes=vmem_limit, collective_id=0, has_side_effects=True
        ),
        cost_estimate=pl.CostEstimate(
            flops=3 * 2 * channels * rows * columns * 700, bytes_accessed=20 * channels * rows * columns, transcendentals=0
        ),
    )(*operands)


def shrink_kernel(dual, update, out):
    total = jnp.zeros(dual.shape[1:], jnp.float32)
    for channel in range(dual.shape[0]):
        lifted = dual[channel] + dual_step * update[channel]
        out[channel] = lifted
        total = total + lifted * lifted
    factor = 1.0 / jnp.maximum(1.0, jnp.sqrt(total) / ball_radius)
    for channel in range(dual.shape[0]):
        out[channel] = out[channel] * factor


def shrink(dual, update):
    channels, rows, width = dual.shape
    block = pl.BlockSpec((channels, 8, width), lambda r: (0, r, 0))
    return pl.pallas_call(
        shrink_kernel,
        name="shrink",
        grid=(rows // 8,),
        in_specs=[block, block],
        out_specs=block,
        out_shape=jax.ShapeDtypeStruct(dual.shape, jnp.float32),
        compiler_params=pltpu.CompilerParams(vmem_limit_bytes=vmem_limit),
        cost_estimate=pl.CostEstimate(flops=5 * dual.size, bytes_accessed=12 * dual.size, transcendentals=0),
    )(dual, update)


def shards(sky_image, measured_real, measured_imaginary, sampling_mask, dual_field):
    channels, rows, columns = sky_image.shape
    facets = lax.axis_size("fac")
    local_dual = lax.all_to_all(dual_field, "fac", split_axis=0, concat_axis=0, tiled=True)
    gradient = data_gradient(sky_image, measured_real, measured_imaginary, sampling_mask)
    next_image, update = primal_step_and_analysis(
        sky_image, gradient, local_dual.reshape(facets, channels, rows, columns // facets)
    )
    return (next_image, shrink(dual_field, update.reshape(dual_field.shape)))


def solution(mesh):
    return jax.shard_map(
        shards,
        mesh=mesh,
        in_specs=(
            P(("groups", "fac"), None, None),
            P(("groups", "fac"), None, None),
            P(("groups", "fac"), None, None),
            P(("groups", "fac"), None, None),
            P("groups", None, "fac"),
        ),
        out_specs=(P(("groups", "fac"), None, None), P("groups", None, "fac")),
        check_vma=False,
    )
```

```python
import jax
import jax.numpy as jnp
import ml_dtypes
import numpy as np
from jax import lax
from jax.experimental import pallas as pl
from jax.experimental.pallas import tpu as pltpu
from jax.sharding import PartitionSpec as P

LEVELS = 4
LANES = 128


low_pass = (
    0.2303778133088964,
    0.7148465705529155,
    0.6308807679298587,
    -0.0279837694168599,
    -0.1870348117190931,
    0.0308413818355607,
    0.0328830116668852,
    -0.010597401785069,
)
high_pass = tuple(((-1) ** tap_index * low_pass[7 - tap_index] for tap_index in range(8)))
primal_step = 0.6
dual_step = 0.8
ball_radius = 12.0
vmem_limit = 48 * 1024 * 1024


def split_table(matrix):
    high = np.asarray(matrix, np.float32).astype(ml_dtypes.bfloat16)
    low = (matrix - high.astype(np.float64)).astype(np.float32).astype(ml_dtypes.bfloat16)
    return [jnp.asarray(high), jnp.asarray(low)]


def halves(values):
    high = values.astype(jnp.bfloat16)
    return high, (values - high.astype(jnp.float32)).astype(jnp.bfloat16)


def dot(left, right):
    return jnp.dot(left, right, preferred_element_type=jnp.float32)


def times_table(values, high_ref, low_ref):
    high, low = halves(values)
    return dot(high, high_ref[...]) + (dot(low, high_ref[...]) + dot(high, low_ref[...]))


def table_times(high_ref, low_ref, values):
    high, low = halves(values)
    return dot(high_ref[...], high) + (dot(high_ref[...], low) + dot(low_ref[...], high))


def dft_angles(length):
    grid = np.arange(length)
    return 2.0 * np.pi * (np.outer(grid, grid) % length) / length


def row_tables(rows):
    angles = dft_angles(rows)
    cosine, sine = np.cos(angles) / np.sqrt(rows), np.sin(angles) / np.sqrt(rows)
    return np.concatenate([cosine, -sine], 0), np.concatenate([cosine, -sine], 1)


def lane_tables(tiles):
    lanes = np.arange(LANES)
    point = (LANES // tiles) * (lanes % tiles) + lanes // tiles
    angles = dft_angles(LANES)[point] / 1.0
    scale = 1.0 / np.sqrt(LANES * tiles)
    cosine, sine = np.cos(angles) * scale, np.sin(angles) * scale
    forward = np.block([[cosine, -sine], [sine, cosine]])
    backward = np.block([[cosine.T, sine.T], [-sine.T, cosine.T]])
    return forward, backward


def twist_table(tiles):
    angles = 2.0 * np.pi * np.outer(np.arange(tiles), np.arange(LANES)) / (tiles * LANES)
    both = np.concatenate([np.cos(angles), np.sin(angles)], 1)
    return jnp.asarray(np.repeat(both[:, None, :], 8, 1), jnp.float32)


def transform(points, sign):
    count = len(points)
    if count == 1:
        return points
    even = transform(points[0::2], sign)
    odd = transform(points[1::2], sign)
    half = count // 2
    first, second = [], []
    for index in range(half):
        real, imag = odd[index]
        if index == 0:
            pass
        elif 4 * index == count:
            real, imag = (-sign * imag, sign * real) if sign > 0 else (imag, -real)
        elif 8 * index == count:
            root = float(np.sqrt(0.5))
            real, imag = (
                ((real - imag) * root, (imag + real) * root)
                if sign > 0
                else ((real + imag) * root, (imag - real) * root)
            )
        elif 8 * index == 3 * count:
            root = float(np.sqrt(0.5))
            real, imag = (
                ((-real - imag) * root, (real - imag) * root)
                if sign > 0
                else ((imag - real) * root, (-real - imag) * root)
            )
        else:
            cosine = float(np.cos(2.0 * np.pi * index / count))
            sine = float(sign * np.sin(2.0 * np.pi * index / count))
            real, imag = real * cosine - imag * sine, real * sine + imag * cosine
        first.append((even[index][0] + real, even[index][1] + imag))
        second.append((even[index][0] - real, even[index][1] - imag))
    return first + second


def turn(slabs):
    slabs = list(slabs)
    lane = lax.broadcasted_iota(jnp.int32, slabs[0].shape, 1)
    step = 1
    while step < len(slabs):
        marked = (lane & step) != 0
        for low in range(len(slabs)):
            if low & step:
                continue
            one, other = slabs[low], slabs[low + step]
            slabs[low] = jnp.where(marked, pltpu.roll(other, step, 1), one)
            slabs[low + step] = jnp.where(marked, other, pltpu.roll(one, LANES - step, 1))
        step *= 2
    return slabs


def gradient_of(
    channel, sky, meas_re, meas_im, mask, row_fh, row_fl, row_bh, row_bl,
    lane_fh, lane_fl, lane_bh, lane_bl, twist, out, field, real_field,
):
    tiles, rows, _ = real_field.shape
    group = 4

    def tile(index):
        return pl.ds(index * LANES, LANES)

    def turn_in(step, carry):
        here = pl.ds(pl.multiple_of(step * 8, 8), 8)
        for index, slab in enumerate(turn([sky[channel, here, tile(t)] for t in range(tiles)])):
            real_field[index, here, :] = slab
        return carry

    lax.fori_loop(0, rows // 8, turn_in, 0)

    def forward(step, carry):
        slabs = [real_field[step * group + i] for i in range(group)]
        both = table_times(row_fh, row_fl, jnp.concatenate(slabs, 1))
        parts = [
            jnp.concatenate([both[:rows, i * LANES : (i + 1) * LANES], both[rows:, i * LANES : (i + 1) * LANES]], 1)
            for i in range(group)
        ]
        result = times_table(jnp.concatenate(parts, 0), lane_fh, lane_fl)
        for i in range(group):
            field[step * group + i] = result[i * rows : (i + 1) * rows]
        return carry

    lax.fori_loop(0, tiles // group, forward, 0)

    def middle(step, carry):
        here = pl.ds(pl.multiple_of(step * 8, 8), 8)
        points = []
        for t in range(tiles):
            real, imag = field[t, here, :LANES], field[t, here, LANES:]
            cosine, sine = twist[t, :, :LANES], twist[t, :, LANES:]
            points.append((real * cosine + imag * sine, imag * cosine - real * sine))
        spectrum = transform(points, -1.0)
        misfit = []
        for t in range(tiles):
            weight = mask[channel, here, tile(t)].astype(jnp.float32)
            misfit.append(
                (
                    weight * (spectrum[t][0] - meas_re[channel, here, tile(t)]),
                    weight * (spectrum[t][1] - meas_im[channel, here, tile(t)]),
                )
            )
        for t, (real, imag) in enumerate(transform(misfit, 1.0)):
            cosine, sine = twist[t, :, :LANES], twist[t, :, LANES:]
            field[t, here, :LANES] = real * cosine - imag * sine
            field[t, here, LANES:] = real * sine + imag * cosine
        return carry

    lax.fori_loop(0, rows // 8, middle, 0)

    def backward(step, carry):
        parts = jnp.concatenate([field[step * group + i] for i in range(group)], 0)
        result = times_table(parts, lane_bh, lane_bl)
        real = [result[i * rows : (i + 1) * rows, :LANES] for i in range(group)]
        imag = [result[i * rows : (i + 1) * rows, LANES:] for i in range(group)]
        both = jnp.concatenate([jnp.concatenate(real, 1), jnp.concatenate(imag, 1)], 0)
        result = table_times(row_bh, row_bl, both)
        for i in range(group):
            real_field[step * group + i] = result[:, i * LANES : (i + 1) * LANES]
        return carry

    lax.fori_loop(0, tiles // group, backward, 0)

    def turn_out(step, carry):
        here = pl.ds(pl.multiple_of(step * 8, 8), 8)
        for index, slab in enumerate(turn([real_field[t, here, :] for t in range(tiles)])):
            out[here, tile(index)] = slab
        return carry

    lax.fori_loop(0, rows // 8, turn_out, 0)


def gradient_tables(rows, columns):
    tiles = columns // LANES
    row_forward, row_backward = row_tables(rows)
    lane_forward, lane_backward = lane_tables(tiles)
    return (
        split_table(row_forward)
        + split_table(row_backward)
        + split_table(lane_forward)
        + split_table(lane_backward)
        + [twist_table(tiles)]
    )


def row_matrix(length):
    current = np.eye(length)
    details = []
    for level_index in range(LEVELS):
        width_now = current.shape[0]
        half_size = width_now // 2
        lower = np.zeros((half_size, width_now))
        upper = np.zeros((half_size, width_now))
        for target in range(half_size):
            for tap_index in range(8):
                lower[target, (2 * target + tap_index) % width_now] += low_pass[tap_index]
                upper[target, (2 * target + tap_index) % width_now] += high_pass[tap_index]
        details.insert(0, upper @ current)
        current = lower @ current
    return np.concatenate([current] + details, 0)


def facet_matrix(width):
    long = 4 * width
    full = row_matrix(long)
    picked = []
    start, size = 0, width >> LEVELS
    for level_index in range(LEVELS + 1):
        picked.append(full[start : start + size])
        start = (long >> LEVELS) << level_index
        size = (width >> LEVELS) << level_index
    block = np.concatenate(picked, 0)
    assert np.all(block[:, 2 * width :] == 0.0)
    return block[:, : 2 * width].T


def step_kernel(*refs):
    images_hbm, dual, fourier = refs[:4], refs[4], refs[5:14]
    row_sh, row_sl, row_ah, row_al, col_sh, col_sl, col_ah, col_al = refs[14:22]
    next_image, received = refs[22:24]
    images = refs[24:28]
    gradient, field, real_field, coefficients, turned, analysed = refs[28:34]
    load_sem, first_send, first_recv, second_send, second_recv, own_sem = refs[34:]
    sky = images[0]
    facets, channels, rows, width = coefficients.shape
    group = 4
    chunks = facets // group
    me = lax.axis_index("fac")
    mesh_id = pl.DeviceIdType.MESH

    def load(index, channel):
        return pltpu.make_async_copy(
            images_hbm[index].at[channel], images[index].at[channel], load_sem.at[index, channel]
        )

    for channel in range(channels):
        for index in range(4):
            load(index, channel).start()

    barrier = pltpu.get_barrier_semaphore()

    def greet(shift, carry):
        pl.semaphore_signal(
            barrier, inc=1, device_id={"fac": (me + shift) % facets}, device_id_type=mesh_id
        )
        return carry

    lax.fori_loop(1, facets, greet, 0)
    pl.semaphore_wait(barrier, facets - 1)

    def first_copy(channel, shift):
        facet = (me + shift) % facets
        return pltpu.make_async_remote_copy(
            src_ref=dual.at[facet, channel],
            dst_ref=coefficients.at[me, channel],
            send_sem=first_send.at[channel, shift],
            recv_sem=first_recv.at[channel, shift],
            device_id={"fac": facet},
            device_id_type=mesh_id,
        )

    def second_copy(channel, facet, shift):
        return pltpu.make_async_remote_copy(
            src_ref=analysed.at[facet, channel],
            dst_ref=received.at[me, channel],
            send_sem=second_send.at[channel, shift],
            recv_sem=second_recv.at[channel, shift],
            device_id={"fac": facet},
            device_id_type=mesh_id,
        )

    for channel in range(channels):

        def send(turn_index, carry, channel=channel):
            odd = turn_index % 2
            shift = odd * ((turn_index + 1) // 2) + (1 - odd) * (facets // 2 + turn_index // 2)
            first_copy(channel, shift).start()
            return carry

        lax.fori_loop(0, facets - 1, send, 0)
    own = pltpu.make_async_copy(dual.at[me], coefficients.at[me], own_sem.at[0])
    own.start()
    own.wait()

    def chunk_at(step):
        return (me // group + chunks // 2 + step) % chunks

    def primal(channel, step):
        chunk = chunk_at(step)
        here = pl.ds(pl.multiple_of(chunk * (group * width), group * width), group * width)
        parts = []
        for i in range(group):
            index = chunk * group + i
            parts.append(
                jnp.concatenate(
                    [coefficients[index, channel], coefficients[(index + facets - 1) % facets, channel]], 1
                )
            )
        prior = times_table(jnp.concatenate(parts, 0), col_sh, col_sl)
        prior = jnp.concatenate([prior[i * rows : (i + 1) * rows] for i in range(group)], 1)
        prior = table_times(row_sh, row_sl, prior)
        old = sky[channel, :, here]
        new = jnp.maximum(old - primal_step * (gradient[:, here] + prior), 0.0)
        next_image[channel, :, here] = new
        result = table_times(row_ah, row_al, 2.0 * new - old)
        for i in range(group):
            turned[chunk * group + i] = result[:, i * width : (i + 1) * width]

    def columns(channel, step):
        chunk = chunk_at(step)
        parts = []
        for i in range(group):
            index = chunk * group + i
            parts.append(jnp.concatenate([turned[index], turned[(index + 1) % facets]], 1))
        result = times_table(jnp.concatenate(parts, 0), col_ah, col_al)
        for i in range(group):
            facet = chunk * group + i
            analysed[facet, channel] = result[i * rows : (i + 1) * rows]

            @pl.when(facet != me)
            def _():
                second_copy(channel, facet, (facet - me + facets) % facets).start()

    for channel in range(channels):
        for index in range(4):
            load(index, channel).wait()
        gradient_of(channel, *images, *fourier, gradient, field, real_field)

        def arrive(shift, carry, channel=channel):
            pltpu.make_async_remote_copy(
                src_ref=dual.at[(me + shift) % facets, channel],
                dst_ref=coefficients.at[(me + facets - shift) % facets, channel],
                send_sem=first_send.at[channel, shift],
                recv_sem=first_recv.at[channel, shift],
                device_id={"fac": (me + shift) % facets},
                device_id_type=mesh_id,
            ).wait_recv()
            return carry

        lax.fori_loop(1, facets, arrive, 0)
        primal(channel, 0)

        def both(step, carry, channel=channel):
            primal(channel, step)
            columns(channel, step - 1)
            return carry

        lax.fori_loop(1, chunks, both, 0)
        columns(channel, chunks - 1)

    own = pltpu.make_async_copy(analysed.at[me], received.at[me], own_sem.at[1])
    own.start()
    own.wait()

    for channel in range(channels):

        def finish(shift, carry, channel=channel):
            to = (me + shift) % facets
            first_copy(channel, shift).wait_send()
            second_copy(channel, to, shift).wait_send()
            pltpu.make_async_remote_copy(
                src_ref=analysed.at[to, channel],
                dst_ref=received.at[(me + facets - shift) % facets, channel],
                send_sem=second_send.at[channel, shift],
                recv_sem=second_recv.at[channel, shift],
                device_id={"fac": to},
                device_id_type=mesh_id,
            ).wait_recv()
            return carry

        lax.fori_loop(1, facets, finish, 0)


def primal_dual_step(sky_image, measured_real, measured_imaginary, sampling_mask, dual):
    channels, rows, columns = sky_image.shape
    facets, width = dual.shape[0], dual.shape[3]
    row_analysis = row_matrix(rows)
    col_analysis = facet_matrix(width)
    col_synthesis = np.concatenate([col_analysis[:width].T, col_analysis[width:].T], 0)
    tables = (
        gradient_tables(rows, columns)
        + split_table(row_analysis.T)
        + split_table(row_analysis)
        + split_table(col_synthesis)
        + split_table(col_analysis)
    )
    images = [sky_image, measured_real, measured_imaginary, sampling_mask]
    vmem, anywhere = pl.BlockSpec(memory_space=pltpu.VMEM), pl.BlockSpec(memory_space=pl.ANY)
    pairs = pltpu.SemaphoreType.DMA((channels, facets))
    return pl.pallas_call(
        step_kernel,
        name="step",
        in_specs=[anywhere] * 5 + [vmem] * len(tables),
        out_specs=[vmem, anywhere],
        out_shape=[
            jax.ShapeDtypeStruct(sky_image.shape, jnp.float32),
            jax.ShapeDtypeStruct(dual.shape, jnp.float32),
        ],
        scratch_shapes=[pltpu.VMEM(image.shape, image.dtype) for image in images]
        + [
            pltpu.VMEM((rows, columns), jnp.float32),
            pltpu.VMEM((columns // LANES, rows, 2 * LANES), jnp.float32),
            pltpu.VMEM((columns // LANES, rows, LANES), jnp.float32),
            pltpu.VMEM(dual.shape, jnp.float32),
            pltpu.VMEM((facets, rows, width), jnp.float32),
            pltpu.VMEM(dual.shape, jnp.float32),
            pltpu.SemaphoreType.DMA((4, channels)),
            pairs,
            pairs,
            pairs,
            pairs,
            pltpu.SemaphoreType.DMA((2,)),
        ],
        compiler_params=pltpu.CompilerParams(
            vmem_limit_bytes=vmem_limit, collective_id=0, has_side_effects=True
        ),
        cost_estimate=pl.CostEstimate(
            flops=3 * 2 * channels * rows * columns * 2100, bytes_accessed=32 * channels * rows * columns, transcendentals=0
        ),
    )(*images, dual, *tables)


def shrink_kernel(dual, update, out):
    total = jnp.zeros(dual.shape[1:], jnp.float32)
    for channel in range(dual.shape[0]):
        lifted = dual[channel] + dual_step * update[channel]
        out[channel] = lifted
        total = total + lifted * lifted
    factor = 1.0 / jnp.maximum(1.0, jnp.sqrt(total) / ball_radius)
    for channel in range(dual.shape[0]):
        out[channel] = out[channel] * factor


def shrink(dual, update):
    channels, rows, width = dual.shape
    block = pl.BlockSpec((channels, 16, width), lambda r: (0, r, 0))
    return pl.pallas_call(
        shrink_kernel,
        name="shrink",
        grid=(rows // 16,),
        in_specs=[block, block],
        out_specs=block,
        out_shape=jax.ShapeDtypeStruct(dual.shape, jnp.float32),
        compiler_params=pltpu.CompilerParams(vmem_limit_bytes=vmem_limit),
        cost_estimate=pl.CostEstimate(flops=5 * dual.size, bytes_accessed=12 * dual.size, transcendentals=0),
    )(dual, update)


def shards(sky_image, measured_real, measured_imaginary, sampling_mask, dual_field):
    channels, rows, columns = sky_image.shape
    facets = lax.axis_size("fac")
    next_image, update = primal_dual_step(
        sky_image,
        measured_real,
        measured_imaginary,
        sampling_mask,
        dual_field.reshape(facets, channels, rows, columns // facets),
    )
    return (next_image, shrink(dual_field, update.reshape(dual_field.shape)))


def solution(mesh):
    return jax.shard_map(
        shards,
        mesh=mesh,
        in_specs=(
            P(("groups", "fac"), None, None),
            P(("groups", "fac"), None, None),
            P(("groups", "fac"), None, None),
            P(("groups", "fac"), None, None),
            P("groups", None, "fac"),
        ),
        out_specs=(P(("groups", "fac"), None, None), P("groups", None, "fac")),
        check_vma=False,
    )
```
